32 devices in a mesh: band: 2 (over x), tm: 16 (over z, y, core).
Axes of the slice: x: 2, y: 2, z: 4, core: 2. Of those that a mesh axis runs over, the one named last changes fastest.
Arguments:
- voltages: bfloat16 [65536, 2048], P(('band', 'tm')), parts along dimension 0, may hold values from -6 to 6
- panel_map: int32 [2048], replicated, may hold values from 0 to 2047, each once
- block_list: int32 [16, 2], replicated, may hold values from 0 to 15, as said below
Outputs:
- visibilities: float32 [32, 2, 256, 128, 128], P('band', None, 'tm'), parts along dimension 0
The draws below stay inside these ranges and needn't reach their ends.
There are 2 independent parts, one for each index of `band`. The reference program is written for one: setup_inputs(seed, part) draws one part's arguments, and reference() takes and returns one part's arrays. A program takes and returns all parts, laid end to end along the dimension named above; an argument that names none is the same for every part. Nothing has to cross between parts.
Inputs may be any that keep to these rules, and one draw needn't show every extreme that they name: `block_list`: each row is a pair of panel numbers; the list names exactly 8 distinct panels, among them panel 0 and panel 16 - 1, every one of them in its first column.
All inputs are finite; a program needn't handle non-finite values.
Results may differ from the reference program's by a relative error of at most 0.0064.
Values may be sent and summed in bfloat16 or wider, within the bound.
A program may use at most 128 MiB of HBM per device.

```python
import jax
import jax.numpy as jnp
from jax import lax

CHANNELS = 256
TAPS = 4
INP = 2048
PANEL = 128
USED = 8
NB = 16
PANELS = 16
SPECTRA = 64
SAMPLES = 32768


def draw_block_list(key, part):
    first_key = jax.random.fold_in(key, 11)
    second_key = jax.random.fold_in(key, 12)
    third_key = jax.random.fold_in(key, 13)
    middle = 1 + jax.random.permutation(first_key, PANELS - 2)[:USED - 2]
    ends_low = jnp.zeros((1,), jnp.int32)
    ends_high = jnp.full((1,), PANELS - 1, jnp.int32)
    picked = jnp.concatenate([ends_low, middle.astype(jnp.int32), ends_high], axis=0)
    chosen = jax.random.permutation(third_key, picked)
    picks = jax.random.randint(second_key, (NB,), 0, USED)
    cycle = jnp.arange(NB) % USED
    return jnp.stack([chosen[cycle], chosen[picks]], axis=1).astype(jnp.int32)


def level_of(own_key, shape, cuts, smallest, top_value):
    level = 1.0
    for axis_at, blocks in cuts:
        draws = jax.random.uniform(jax.random.fold_in(jax.random.fold_in(own_key, 6), axis_at), (blocks,), jnp.float32, smallest / len(cuts), top_value / len(cuts))
        level = level * jnp.repeat(jnp.exp(draws), shape[axis_at] // blocks).reshape((-1,) + (1,) * (len(shape) - 1 - axis_at))
    return level


def normal_values(key, dims, deviation, limit, split=(), kind=jnp.bfloat16):
    values = jax.random.normal(key, dims, jnp.float32) * deviation
    if len(split) > 0:
        values = level_of(key, dims, split, -0.22, 0.18) * values
    return jnp.clip(values, min=-limit, max=limit).astype(kind)


def setup_inputs(seed: int = 0, part: int = 0) -> dict:
    seeds = jax.random.split(jax.random.key(seed), 4)
    part_keys = jax.random.split(jax.random.fold_in(seeds[3], part), 4)
    voltages = normal_values(part_keys[0], (SAMPLES, INP), 1.0, 6.0, ((0, 16),))
    panel_map = jax.random.permutation(seeds[1], INP).astype(jnp.int32)
    block_list = draw_block_list(jax.random.fold_in(seeds[3], 71), part)
    return {"voltages": voltages, "panel_map": panel_map, "block_list": block_list}


def filter_taps(taps, frame):
    length = taps * frame
    place = jnp.arange(length).astype(jnp.float32)
    middle = (length - 1) / 2.0
    window = 0.5 - 0.5 * jnp.cos(2.0 * jnp.pi * (place + 0.5) / length)
    shape_h = jnp.sinc((place - middle) / frame) * window
    shape_h = shape_h / jnp.sqrt(jnp.sum(shape_h * shape_h))
    return shape_h.reshape(taps, frame).astype(jnp.float32)

def dft_table(channels):
    frame = 2 * channels
    rows_k = jnp.arange(channels, dtype=jnp.int32)[:, None]
    cols_n = jnp.arange(frame, dtype=jnp.int32)[None, :]
    phase = (rows_k * cols_n % frame).astype(jnp.float32) * (2.0 * jnp.pi / frame)
    return jnp.concatenate([jnp.cos(phase), -jnp.sin(phase)], axis=0).astype(jnp.bfloat16)

def reference(voltages, panel_map, block_list):
    frame = 2 * CHANNELS
    frames = voltages.reshape(SPECTRA, frame, INP)
    padded = jnp.concatenate([jnp.zeros((TAPS - 1, frame, INP), voltages.dtype), frames], axis=0)
    coeff = filter_taps(TAPS, frame)
    filtered = jnp.zeros((SPECTRA, frame, INP), jnp.float32)
    for tap in range(TAPS):
        filtered = filtered + coeff[tap][None, :, None] * padded[tap:tap + SPECTRA].astype(jnp.float32)
    filtered = filtered.astype(jnp.bfloat16)
    table = dft_table(CHANNELS)
    spectra = jnp.einsum('kn,sni->ski', table.astype(jnp.float32), filtered.astype(jnp.float32))
    spectra = spectra.astype(jnp.bfloat16).reshape(SPECTRA, 2, CHANNELS, INP)
    columns = panel_map.reshape(PANELS, PANEL)[block_list]

    def one_block(pair):
        first = spectra[:, :, :, pair[0]].astype(jnp.float32)
        second = spectra[:, :, :, pair[1]].astype(jnp.float32)
        flipped = jnp.stack([first[:, 1], -first[:, 0]], axis=1)
        real_part = jnp.einsum('scfi,scfj->fij', first, second)
        imag_part = jnp.einsum('scfi,scfj->fij', flipped, second)
        return jnp.stack([real_part, imag_part], axis=0) / SPECTRA
    return lax.map(one_block, columns)
```

```python
import functools

import jax
import jax.numpy as jnp
import ml_dtypes
import numpy as np
from jax import lax
from jax.experimental import pallas as pl
from jax.experimental.pallas import tpu as pltpu
from jax.sharding import PartitionSpec as P

CHANNELS = 256
TAPS = 4
PANEL = 128
USED = 8
WIDE = 256
MESH = pl.DeviceIdType.MESH


def filter_taps(taps, frame):
    length = taps * frame
    place = np.arange(length).astype(np.float64)
    middle = (length - 1) / 2.0
    window = 0.5 - 0.5 * np.cos(2.0 * np.pi * (place + 0.5) / length)
    shape_h = np.sinc((place - middle) / frame) * window
    shape_h = shape_h / np.sqrt(np.sum(shape_h * shape_h))
    return shape_h.reshape(taps, frame).astype(np.float32)


def dft_table(channels):
    frame = 2 * channels
    rows_k = np.arange(channels)[:, None]
    cols_n = np.arange(frame)[None, :]
    phase = (rows_k * cols_n % frame) * (2.0 * np.pi / frame)
    table = np.stack([np.cos(phase), -np.sin(phase)], axis=0)
    return table.astype(ml_dtypes.bfloat16).astype(np.float32)


def filterbank_matrix(spec_dev):
    frame = 2 * CHANNELS
    coeff = filter_taps(TAPS, frame)
    table = dft_table(CHANNELS)
    padded = spec_dev + TAPS - 1
    full = np.zeros((CHANNELS, spec_dev, 2, padded, frame), np.float32)
    for s in range(spec_dev):
        for t in range(TAPS):
            full[:, s, :, s + t, :] = np.moveaxis(table * coeff[t], 0, 1)
    return full.reshape(CHANNELS * spec_dev * 2, padded * frame).astype(ml_dtypes.bfloat16)


def regroup_matrix(sources, spec_dev):
    per = 2 * spec_dev
    pair = 16 // per
    out = np.zeros((pair, 2, sources, spec_dev, 2, sources, pair, spec_dev, 2), np.float32)
    for f in range(pair):
        for g in range(sources):
            for s in range(spec_dev):
                out[f, 0, g, s, 0, g, f, s, 0] = 1
                out[f, 0, g, s, 1, g, f, s, 1] = 1
                out[f, 1, g, s, 0, g, f, s, 1] = 1
                out[f, 1, g, s, 1, g, f, s, 0] = -1
    return out.reshape(pair, 2, sources * per, sources * 16).astype(ml_dtypes.bfloat16)


def exchange_kernel(n, chunks, volt_hbm, mat_hbm, cols_ref, data_ref, volt, mat, onehot,
                    padded, spectra, load_sem, halo_send, halo_recv, own_sem, send_sem, recv_sem):
    me = lax.axis_index("tm")
    rows, width = volt.shape
    head = padded.shape[1] - rows
    total = spectra.shape[1]
    block = total // n
    tile = 512
    load_v = pltpu.make_async_copy(volt_hbm, volt, load_sem.at[0])
    load_m = pltpu.make_async_copy(mat_hbm, mat, load_sem.at[1])
    load_v.start()
    load_m.start()
    barrier = pltpu.get_barrier_semaphore()

    def greet(k, carry):
        peer = lax.rem(me + k, n)
        pl.semaphore_signal(barrier, inc=1, device_id={"tm": peer}, device_id_type=MESH)
        return carry

    lax.fori_loop(1, n, greet, 0)

    def select(c):
        cols = cols_ref[:, c * WIDE : (c + 1) * WIDE]

        def mark(i, carry):
            at = pl.multiple_of(i * 256, 256)
            place = lax.broadcasted_iota(jnp.int32, (256, WIDE), 0) + at
            onehot[pl.ds(at, 256), :] = jnp.where(place == cols, 1.0, 0.0).astype(jnp.bfloat16)
            return carry

        lax.fori_loop(0, width // 256, mark, 0)
        if c == 0:
            load_v.wait()

        def pick(i, carry):
            at = pl.multiple_of(i * tile, tile)
            got = jnp.dot(volt[pl.ds(at, tile), :], onehot[...], preferred_element_type=jnp.float32)
            padded[c, pl.ds(pl.multiple_of(head + at, tile), tile), :] = got.astype(jnp.bfloat16)
            return carry

        lax.fori_loop(0, rows // tile, pick, 0)

    def halo(c):
        return pltpu.make_async_remote_copy(
            src_ref=padded.at[c, pl.ds(rows, head), :],
            dst_ref=padded.at[c, pl.ds(0, head), :],
            send_sem=halo_send.at[c],
            recv_sem=halo_recv.at[c],
            device_id={"tm": lax.rem(me + 1, n)},
            device_id_type=MESH,
        )

    def send_halo(c):
        @pl.when(me < n - 1)
        def _():
            halo(c).start()

    def piece(c, k):
        peer = lax.rem(me + k, n)
        return pltpu.make_async_remote_copy(
            src_ref=spectra.at[c, pl.ds(pl.multiple_of(peer * block, block), block), :],
            dst_ref=data_ref.at[c, me],
            send_sem=send_sem.at[c, k],
            recv_sem=recv_sem.at[c, k],
            device_id={"tm": peer},
            device_id_type=MESH,
        )

    def own(c):
        return pltpu.make_async_copy(
            spectra.at[c, pl.ds(pl.multiple_of(me * block, block), block), :],
            data_ref.at[c, me],
            own_sem.at[c],
        )

    def channelize(c):
        @pl.when(me > 0)
        def _():
            halo(c).wait_recv()

        @pl.when(me == 0)
        def _():
            padded[c, pl.ds(0, head), :] = jnp.zeros((head, WIDE), jnp.bfloat16)

        if c == 0:
            load_m.wait()

        def run(i, carry):
            at = pl.multiple_of(i * tile, tile)
            got = jnp.dot(mat[pl.ds(at, tile), :], padded[c], preferred_element_type=jnp.float32)
            spectra[c, pl.ds(at, tile), :] = got.astype(jnp.bfloat16)
            return carry

        lax.fori_loop(0, total // tile, run, 0)

    def send(c):
        def one(k, carry):
            piece(c, k).start()
            return carry

        lax.fori_loop(1, n, one, 0)
        own(c).start()

    ahead = min(2, chunks)
    for c in range(ahead):
        select(c)
        if c == 0:
            pl.semaphore_wait(barrier, n - 1)
        send_halo(c)
    for c in range(chunks):
        channelize(c)
        send(c)
        if c + ahead < chunks:
            select(c + ahead)
            send_halo(c + ahead)
    for c in range(chunks):
        @pl.when(me < n - 1)
        def _():
            halo(c).wait_send()

        own(c).wait()

        def finish(k, carry):
            piece(c, k).wait()
            return carry

        lax.fori_loop(1, n, finish, 0)


def exchange(voltages, matrix, cols, n):
    rows, width = voltages.shape
    total, depth = matrix.shape
    chunks = cols.shape[1] // WIDE
    block = total // n
    return pl.pallas_call(
        functools.partial(exchange_kernel, n, chunks),
        out_shape=jax.ShapeDtypeStruct((chunks, n, block, WIDE), jnp.bfloat16),
        in_specs=[
            pl.BlockSpec(memory_space=pl.ANY),
            pl.BlockSpec(memory_space=pl.ANY),
            pl.BlockSpec(memory_space=pltpu.VMEM),
        ],
        out_specs=pl.BlockSpec(memory_space=pl.ANY),
        scratch_shapes=[
            pltpu.VMEM((rows, width), jnp.bfloat16),
            pltpu.VMEM((total, depth), jnp.bfloat16),
            pltpu.VMEM((width, WIDE), jnp.bfloat16),
            pltpu.VMEM((chunks, depth, WIDE), jnp.bfloat16),
            pltpu.VMEM((chunks, total, WIDE), jnp.bfloat16),
            pltpu.SemaphoreType.DMA((2,)),
            pltpu.SemaphoreType.DMA((chunks,)),
            pltpu.SemaphoreType.DMA((chunks,)),
            pltpu.SemaphoreType.DMA((chunks,)),
            pltpu.SemaphoreType.DMA((chunks, n)),
            pltpu.SemaphoreType.DMA((chunks, n)),
        ],
        compiler_params=pltpu.CompilerParams(
            collective_id=0, has_side_effects=True, vmem_limit_bytes=56 * 1024 * 1024
        ),
        name="channelize_exchange",
    )(voltages, matrix, cols)


def correlate_kernel(scale, slots, data_ref, plain_ref, both_ref, out_ref, lhs, rhs):
    chunks, sources, group, _ = data_ref.shape
    pair = out_ref.shape[2]
    depth = rhs.shape[2]
    per = WIDE // PANEL
    for c in range(chunks):
        got = data_ref[c].reshape(sources * group, WIDE)
        second = jnp.dot(plain_ref[...], got, preferred_element_type=jnp.float32)
        second = second.astype(jnp.bfloat16)
        first = lax.dot_general(
            got, both_ref[...], (((0,), (1,)), ((), ())), preferred_element_type=jnp.float32
        )
        first = (first * scale).astype(jnp.bfloat16)
        for h in range(per):
            for f in range(pair):
                rhs[c * per + h, f] = second[
                    f * depth : (f + 1) * depth, h * PANEL : (h + 1) * PANEL
                ]
                for kind in range(2):
                    at = (f * 2 + kind) * depth
                    lhs[c * per + h, f, kind * PANEL : (kind + 1) * PANEL, :] = first[
                        h * PANEL : (h + 1) * PANEL, at : at + depth
                    ]

    for b in range(out_ref.shape[0]):
        a, w = slots[2 * b], slots[2 * b + 1]
        for f in range(pair):
            got = jnp.dot(lhs[a, f], rhs[w, f], preferred_element_type=jnp.float32)
            out_ref[b, 0, f] = got[:PANEL]
            out_ref[b, 1, f] = got[PANEL:]


def correlate(data, slots, spec_dev, band_dev):
    chunks, sources, block, _ = data.shape
    pair = 16 // (2 * spec_dev)
    depth = sources * spec_dev * 2
    blocks = slots.shape[0] // 2
    regroup = regroup_matrix(sources, spec_dev)
    plain = jnp.asarray(regroup[:, 0].reshape(pair * depth, sources * 16))
    both = jnp.asarray(regroup.reshape(pair * 2 * depth, sources * 16))
    return pl.pallas_call(
        functools.partial(correlate_kernel, 1.0 / (sources * spec_dev)),
        out_shape=jax.ShapeDtypeStruct((blocks, 2, band_dev, PANEL, PANEL), jnp.float32),
        grid_spec=pltpu.PrefetchScalarGridSpec(
            num_scalar_prefetch=1,
            grid=(band_dev // pair,),
            in_specs=[
                pl.BlockSpec((chunks, sources, 16, WIDE), lambda j, s: (0, 0, j, 0)),
                pl.BlockSpec(plain.shape, lambda j, s: (0, 0)),
                pl.BlockSpec(both.shape, lambda j, s: (0, 0)),
            ],
            out_specs=pl.BlockSpec((blocks, 2, pair, PANEL, PANEL), lambda j, s: (0, 0, j, 0, 0)),
            scratch_shapes=[
                pltpu.VMEM((USED, pair, 2 * PANEL, depth), jnp.bfloat16),
                pltpu.VMEM((USED, pair, depth, PANEL), jnp.bfloat16),
            ],
        ),
        compiler_params=pltpu.CompilerParams(vmem_limit_bytes=48 * 1024 * 1024),
        name="correlate",
    )(slots, data, plain, both)


def body(voltages, panel_map, block_list):
    frame = 2 * CHANNELS
    spec_dev = voltages.shape[0] // frame
    groups = lax.axis_size("tm")
    band_dev = CHANNELS // groups
    panels = panel_map.shape[0] // PANEL
    named = jnp.any(block_list.reshape(-1)[:, None] == jnp.arange(panels)[None, :], axis=0)
    before = jnp.arange(panels)[None, :] < jnp.arange(panels)[:, None]
    rank = jnp.sum(jnp.where(before & named[None, :], 1, 0), axis=1)
    at_slot = named[None, :] & (rank[None, :] == jnp.arange(USED)[:, None])
    panel_rows = panel_map.reshape(panels, PANEL)
    cols = jnp.sum(jnp.where(at_slot[:, :, None], panel_rows[None], 0), axis=1)
    flat = block_list.reshape(-1)
    slots = jnp.sum(jnp.where(flat[:, None] == jnp.arange(panels)[None, :], rank[None, :], 0), axis=1)
    matrix = jnp.asarray(filterbank_matrix(spec_dev))
    data = exchange(voltages, matrix, cols.reshape(1, USED * PANEL).astype(jnp.int32), groups)
    return correlate(data, slots.astype(jnp.int32), spec_dev, band_dev)


def solution(mesh):
    in_specs = (P(("band", "tm"), None), P(), P())
    out_specs = P("band", None, "tm", None, None)
    return jax.shard_map(body, mesh=mesh, in_specs=in_specs, out_specs=out_specs, check_vma=False)
```
